256 devices in a mesh: dp: 8 (over z), tok: 2 (over core), expert: 16 (over y, x).
Axes of the slice: x: 4, y: 4, z: 8, core: 2. Of those that a mesh axis runs over, the one named last changes fastest.
Arguments:
- tokens: bfloat16 [256, 256, 1280], P(('dp', 'tok', 'expert')), may hold values from -6 to 6
- router: bfloat16 [1280, 32], replicated, may hold values from -13.975425 to 13.975425
- expert_in: bfloat16 [32, 1280, 5120], P(('tok', 'expert'), None, 'dp'), may hold values from -0.15625 to 0.15625
- expert_out: bfloat16 [32, 5120, 1280], P(('tok', 'expert'), 'dp'), may hold values from -0.078125 to 0.078125
- grad_out: bfloat16 [256, 256, 1280], P(('dp', 'tok', 'expert')), may hold values from -6 to 6
Outputs:
- grad_tokens: bfloat16 [256, 256, 1280], P(('dp', 'tok', 'expert'))
- grad_router: float32 [1280, 32], replicated
- grad_expert_in: bfloat16 [32, 1280, 5120], P(('tok', 'expert'), None, 'dp')
- grad_expert_out: bfloat16 [32, 5120, 1280], P(('tok', 'expert'), 'dp')
The draws below stay inside these ranges and needn't reach their ends.
All inputs are finite; a program needn't handle non-finite values.
Results may differ from the reference program's by a relative error of at most 0.0085.
Values may be sent and summed in bfloat16 or wider, within the bound.
No kernel may reach another device: no remote copies, remote signals or barrier semaphores. Data moves between devices by JAX's collectives and lax.ppermute only.
A program may use at most 64 MiB of HBM per device.

```python
from functools import partial
import jax
import jax.numpy as jnp
from jax import lax

D = 1280
HID = 5120
SEQ = 256
ITERS = 4
EXPERTS = 32
IMAGES = 256


def draw_router(key, part):
    first_key, second_key = jax.random.split(key)
    base_draw = jnp.clip(jax.random.normal(first_key, (D, EXPERTS), jnp.float32), -6.0, 6.0)
    lowest, highest = (0.5, 4.0)
    column_scale = jnp.exp(jax.random.uniform(second_key, (1, EXPERTS), jnp.float32, jnp.log(lowest), jnp.log(highest)))
    return (base_draw * column_scale * D ** (-0.5)).astype(jnp.bfloat16)


def level_of(key, shape, pieces, low, top_value):
    gain, own = 1.0, jax.random.fold_in(key, 6)
    for position, parts in pieces:
        steps = jnp.exp(jax.random.uniform(jax.random.fold_in(own, position), (parts,), jnp.float32, low / len(pieces), top_value / len(pieces)))
        gain = gain * jnp.repeat(steps, shape[position] // parts).reshape([-1 if axis == position else 1 for axis in range(len(shape))])
    return gain


def bell_draw(stream_key, dims, deviation, most, shards=(), dtype=jnp.bfloat16):
    factor_of = level_of(stream_key, dims, shards, -0.22, 0.18) if shards else 1.0
    array = jax.random.normal(stream_key, dims, jnp.float32) * deviation * factor_of
    return jnp.minimum(jnp.maximum(array, -most), most).astype(dtype)


def setup_inputs(seed: int = 0) -> dict:
    key_list = jax.random.split(jax.random.key(seed), 6)
    return {
        "tokens": bell_draw(key_list[0], (IMAGES, SEQ, D), 1.0, 6.0, ((0, 256),)),
        "router": draw_router(jax.random.fold_in(key_list[5], 71), 0),
        "expert_in": bell_draw(key_list[2], (EXPERTS, D, HID), D ** -0.5, 0.15625, ((0, 32), (2, 8))),
        "expert_out": bell_draw(key_list[3], (EXPERTS, HID, D), HID ** -0.5, 0.078125, ((0, 32), (1, 8))),
        "grad_out": bell_draw(key_list[4], (IMAGES, SEQ, D), 1.0, 6.0, ((0, 256),)),
    }


GELU_SCALE = 0.7978845608028654
GELU_CUBIC = 0.044715


def gelu_pair(hidden_pre):
    inner_arg = GELU_SCALE * (hidden_pre + GELU_CUBIC * hidden_pre * hidden_pre * hidden_pre)
    tanh_val = jnp.tanh(inner_arg)
    activated = 0.5 * hidden_pre * (1.0 + tanh_val)
    derivative = 0.5 * (1.0 + tanh_val) + 0.5 * hidden_pre * (1.0 - tanh_val * tanh_val) * GELU_SCALE * (1.0 + 3.0 * GELU_CUBIC * hidden_pre * hidden_pre)
    return activated, derivative


def balancing_iterates(router_scores):
    iterate = router_scores
    stored_residuals = []
    for sweep_index in range(ITERS):
        line_divisor_factor = iterate - jax.nn.logsumexp(iterate, axis=1, keepdims=True)
        column_divisor = line_divisor_factor - jax.nn.logsumexp(line_divisor_factor, axis=0, keepdims=True)
        stored_residuals.append((line_divisor_factor, column_divisor))
        iterate = column_divisor
    return stored_residuals


def image_forward(router, pair_in):
    picture_patches, image_grad = pair_in
    router_scores = jnp.dot(picture_patches, router, preferred_element_type=jnp.float32)
    combine_rounded = jax.nn.softmax(router_scores, axis=1).astype(jnp.bfloat16)
    stored_residuals = balancing_iterates(router_scores)
    dispatch_rounded = jnp.exp(stored_residuals[-1][1]).astype(jnp.bfloat16)
    slot_in = jnp.dot(dispatch_rounded.T, picture_patches, preferred_element_type=jnp.float32).astype(jnp.bfloat16)
    slot_grad = jnp.dot(combine_rounded.T, image_grad, preferred_element_type=jnp.float32).astype(jnp.bfloat16)
    return slot_in, slot_grad


def expert_pass(packed):
    slot_in, slot_grad, weight_in, weight_out = packed
    hidden_pre = jnp.dot(slot_in, weight_in, preferred_element_type=jnp.float32)
    activated, derivative = gelu_pair(hidden_pre)
    hidden_act = activated.astype(jnp.bfloat16)
    slot_out = jnp.dot(hidden_act, weight_out, preferred_element_type=jnp.float32).astype(jnp.bfloat16)
    grad_act = jnp.dot(slot_grad, weight_out.T, preferred_element_type=jnp.float32)
    grad_pre = (grad_act * derivative).astype(jnp.bfloat16)
    bucket_cotangent = jnp.dot(grad_pre, weight_in.T, preferred_element_type=jnp.float32).astype(jnp.bfloat16)
    grad_win = jnp.dot(slot_in.T, grad_pre, preferred_element_type=jnp.float32).astype(jnp.bfloat16)
    out_weight_gradient = jnp.dot(hidden_act.T, slot_grad, preferred_element_type=jnp.float32).astype(jnp.bfloat16)
    return slot_out, bucket_cotangent, grad_win, out_weight_gradient


def image_backward(router, running_total_sum, packed):
    picture_patches, image_grad, slot_out, bucket_cotangent = packed
    router_scores = jnp.dot(picture_patches, router, preferred_element_type=jnp.float32)
    combine = jax.nn.softmax(router_scores, axis=1)
    stored_residuals = balancing_iterates(router_scores)
    assignment_matrix = jnp.exp(stored_residuals[-1][1])
    dispatch_rounded = assignment_matrix.astype(jnp.bfloat16)
    grad_comb = jnp.dot(image_grad, slot_out.T, preferred_element_type=jnp.float32)
    logit_cotangent = combine * (grad_comb - jnp.sum(combine * grad_comb, axis=1, keepdims=True))
    doubly_stochastic_adjoint = jnp.dot(picture_patches, bucket_cotangent.T, preferred_element_type=jnp.float32) * assignment_matrix
    for line_divisor_factor, column_divisor in reversed(stored_residuals):
        doubly_stochastic_adjoint = doubly_stochastic_adjoint - jnp.exp(column_divisor) * jnp.sum(doubly_stochastic_adjoint, axis=0, keepdims=True)
        doubly_stochastic_adjoint = doubly_stochastic_adjoint - jnp.exp(line_divisor_factor) * jnp.sum(doubly_stochastic_adjoint, axis=1, keepdims=True)
    accumulated_cotangent = (logit_cotangent + doubly_stochastic_adjoint).astype(jnp.bfloat16)
    grad_image = (jnp.dot(dispatch_rounded, bucket_cotangent, preferred_element_type=jnp.float32)
                  + jnp.dot(accumulated_cotangent, router.T, preferred_element_type=jnp.float32)).astype(jnp.bfloat16)
    running_total_sum = running_total_sum + jnp.dot(picture_patches.T, accumulated_cotangent, preferred_element_type=jnp.float32)
    return running_total_sum, grad_image


def reference(tokens, router, expert_in, expert_out, grad_out):
    slot_in, slot_grad = lax.map(partial(image_forward, router), (tokens, grad_out))
    slot_out, bucket_cotangent, grad_win, out_weight_gradient = lax.map(
        expert_pass, (jnp.swapaxes(slot_in, 0, 1), jnp.swapaxes(slot_grad, 0, 1), expert_in, expert_out))
    packed = (tokens, grad_out, jnp.swapaxes(slot_out, 0, 1), jnp.swapaxes(bucket_cotangent, 0, 1))

    def scan_step(running_total_sum, packed_one):
        return image_backward(router, running_total_sum, packed_one)

    grad_router, grad_tokens = lax.scan(scan_step, jnp.zeros((D, EXPERTS), jnp.float32), packed)
    return grad_tokens, grad_router, grad_win, out_weight_gradient
```

```python
import jax
import jax.numpy as jnp
from jax import lax
from jax.sharding import PartitionSpec as P

ITERS = 4


GELU_SCALE = 0.7978845608028654
GELU_CUBIC = 0.044715


def gelu_pair(hidden_pre):
    inner_arg = GELU_SCALE * (hidden_pre + GELU_CUBIC * hidden_pre * hidden_pre * hidden_pre)
    tanh_val = jnp.tanh(inner_arg)
    activated = 0.5 * hidden_pre * (1.0 + tanh_val)
    derivative = 0.5 * (1.0 + tanh_val) + 0.5 * hidden_pre * (
        1.0 - tanh_val * tanh_val
    ) * GELU_SCALE * (1.0 + 3.0 * GELU_CUBIC * hidden_pre * hidden_pre)
    return (activated, derivative)


def forward_iterates(router_scores):
    iterate = router_scores
    stored_residuals = []
    for sweep_index in range(ITERS):
        line_divisor_factor = iterate - jax.nn.logsumexp(iterate, axis=1, keepdims=True)
        column_divisor = line_divisor_factor - jax.nn.logsumexp(
            line_divisor_factor, axis=0, keepdims=True
        )
        stored_residuals.append((line_divisor_factor, column_divisor))
        iterate = column_divisor
    return stored_residuals


def backward_sequence(gradient, stored_residuals):
    for line_divisor_factor, column_divisor in reversed(stored_residuals):
        gradient = gradient - jnp.exp(column_divisor) * jnp.sum(gradient, axis=0, keepdims=True)
        gradient = gradient - jnp.exp(line_divisor_factor) * jnp.sum(
            gradient, axis=1, keepdims=True
        )
    return gradient


def shift(value, step):
    size = lax.axis_size("dp")
    return lax.ppermute(value, "dp", [(i, (i + step) % size) for i in range(size)])


def ring_gather(rows):
    half = rows.shape[1] // 2
    blocks = [rows]
    behind = ahead = rows
    for _ in range(3):
        behind, ahead = shift(behind, 1), shift(ahead, -1)
        blocks += [behind, ahead]
    far = jnp.concatenate([shift(behind[:, :half], 1), shift(ahead[:, half:], -1)], axis=1)
    return jnp.concatenate(blocks + [far], axis=0)


def ring_reduce(partial, rows):
    half = partial.shape[1] // 2
    block = [partial[i * rows : (i + 1) * rows] for i in range(8)]
    own, far = block[0], block[7]
    down_path, up_path = [block[5], block[3], block[1]], [block[6], block[4], block[2]]
    narrow = jnp.bfloat16
    wide = jnp.float32
    from_above = shift(far[:, :half].astype(narrow), -1).astype(wide)
    from_below = shift(far[:, half:].astype(narrow), 1).astype(wide)
    down = jnp.concatenate([from_above + down_path[0][:, :half], down_path[0][:, half:]], axis=1)
    up = jnp.concatenate([up_path[0][:, :half], from_below + up_path[0][:, half:]], axis=1)
    for step in range(3):
        down = shift(down.astype(narrow), -1).astype(wide)
        up = shift(up.astype(narrow), 1).astype(wide)
        if step < 2:
            down, up = down + down_path[step + 1], up + up_path[step + 1]
    return own + down + up


def swap(value):
    return lax.all_to_all(value, ("tok", "expert"), split_axis=0, concat_axis=0, tiled=True)


def sum_everywhere(part):
    slots = part.shape[0]
    mine = jnp.sum(swap(part), axis=0, keepdims=True)
    seen = [mine] + [shift(mine, step) for step in range(1, 8)]
    while len(seen) > 1:
        middle = len(seen) // 2
        seen = [seen[i] + seen[i + middle] for i in range(middle)]
    return swap(jnp.broadcast_to(seen[0], (slots, part.shape[1])))


def body(tokens, router, expert_in, expert_out, grad_out):
    patches, image_grad = tokens[0], grad_out[0]
    model_width = patches.shape[1]
    router_scores = jnp.dot(patches, router, preferred_element_type=jnp.float32)
    combine = jax.nn.softmax(router_scores, axis=1)
    combine_rounded = combine.astype(jnp.bfloat16)
    stored_residuals = forward_iterates(router_scores)
    assignment_matrix = jnp.exp(stored_residuals[-1][1])
    dispatch_rounded = assignment_matrix.astype(jnp.bfloat16)
    slot_part = jnp.dot(dispatch_rounded.T, patches, preferred_element_type=jnp.float32).astype(
        jnp.bfloat16
    )
    grad_part = jnp.dot(combine_rounded.T, image_grad, preferred_element_type=jnp.float32).astype(
        jnp.bfloat16
    )
    rows = swap(jnp.concatenate([slot_part, grad_part], axis=1))
    gathered = ring_gather(rows)
    all_in, all_grad = gathered[:, :model_width], gathered[:, model_width:]
    weight_in = expert_in[0]
    weight_out = expert_out[0]
    hidden_pre = jnp.dot(all_in, weight_in, preferred_element_type=jnp.float32)
    activated, derivative = gelu_pair(hidden_pre)
    hidden_act = activated.astype(jnp.bfloat16)
    grad_act = lax.dot_general(
        all_grad, weight_out, (((1,), (1,)), ((), ())), preferred_element_type=jnp.float32
    )
    grad_pre = (grad_act * derivative).astype(jnp.bfloat16)
    forward_rows = jnp.dot(hidden_act, weight_out, preferred_element_type=jnp.float32)
    backward_rows = lax.dot_general(
        grad_pre, weight_in, (((1,), (1,)), ((), ())), preferred_element_type=jnp.float32
    )
    summed = ring_reduce(
        jnp.concatenate([forward_rows, backward_rows], axis=1), rows.shape[0]
    ).astype(jnp.bfloat16)
    grad_win = lax.dot_general(
        all_in, grad_pre, (((0,), (0,)), ((), ())), preferred_element_type=jnp.float32
    ).astype(jnp.bfloat16)[None]
    out_weight_gradient = lax.dot_general(
        hidden_act, all_grad, (((0,), (0,)), ((), ())), preferred_element_type=jnp.float32
    ).astype(jnp.bfloat16)[None]
    back = swap(summed)
    back_out, back_grad = back[:, :model_width], back[:, model_width:]
    grad_comb = lax.dot_general(
        image_grad, back_out, (((1,), (1,)), ((), ())), preferred_element_type=jnp.float32
    )
    logit_cotangent = combine * (grad_comb - jnp.sum(combine * grad_comb, axis=1, keepdims=True))
    doubly_stochastic_adjoint = (
        lax.dot_general(
            patches, back_grad, (((1,), (1,)), ((), ())), preferred_element_type=jnp.float32
        )
        * assignment_matrix
    )
    doubly_stochastic_adjoint = backward_sequence(doubly_stochastic_adjoint, stored_residuals)
    accumulated_cotangent = (logit_cotangent + doubly_stochastic_adjoint).astype(jnp.bfloat16)
    router_part = lax.dot_general(
        accumulated_cotangent, patches, (((0,), (0,)), ((), ())), preferred_element_type=jnp.float32
    )
    grad_router = sum_everywhere(router_part).T
    grad_tokens = (
        jnp.dot(dispatch_rounded, back_grad, preferred_element_type=jnp.float32)
        + lax.dot_general(
            accumulated_cotangent, router, (((1,), (1,)), ((), ())), preferred_element_type=jnp.float32
        )
    ).astype(jnp.bfloat16)[None]
    return (grad_tokens, grad_router, grad_win, out_weight_gradient)


def solution(mesh):
    return jax.shard_map(
        body,
        mesh=mesh,
        in_specs=(
            P(("dp", "tok", "expert"), None, None),
            P(),
            P(("tok", "expert"), None, "dp"),
            P(("tok", "expert"), "dp", None),
            P(("dp", "tok", "expert"), None, None),
        ),
        out_specs=(
            P(("dp", "tok", "expert"), None, None),
            P(),
            P(("tok", "expert"), None, "dp"),
            P(("tok", "expert"), "dp", None),
        ),
        check_vma=False,
    )
```

```python
import jax
import jax.numpy as jnp
from jax import lax
from jax.sharding import PartitionSpec as P

ITERS = 4


GELU_SCALE = 0.7978845608028654
GELU_CUBIC = 0.044715


def gelu_pair(hidden_pre):
    inner_arg = GELU_SCALE * (hidden_pre + GELU_CUBIC * hidden_pre * hidden_pre * hidden_pre)
    tanh_val = jnp.tanh(inner_arg)
    activated = 0.5 * hidden_pre * (1.0 + tanh_val)
    derivative = 0.5 * (1.0 + tanh_val) + 0.5 * hidden_pre * (
        1.0 - tanh_val * tanh_val
    ) * GELU_SCALE * (1.0 + 3.0 * GELU_CUBIC * hidden_pre * hidden_pre)
    return (activated, derivative)


def forward_iterates(router_scores):
    iterate = router_scores
    stored_residuals = []
    for sweep_index in range(ITERS):
        line_divisor_factor = iterate - jax.nn.logsumexp(iterate, axis=1, keepdims=True)
        column_divisor = line_divisor_factor - jax.nn.logsumexp(
            line_divisor_factor, axis=0, keepdims=True
        )
        stored_residuals.append((line_divisor_factor, column_divisor))
        iterate = column_divisor
    return stored_residuals


def backward_sequence(gradient, stored_residuals):
    for line_divisor_factor, column_divisor in reversed(stored_residuals):
        gradient = gradient - jnp.exp(column_divisor) * jnp.sum(gradient, axis=0, keepdims=True)
        gradient = gradient - jnp.exp(line_divisor_factor) * jnp.sum(
            gradient, axis=1, keepdims=True
        )
    return gradient


def shift(value, step):
    size = lax.axis_size("dp")
    return lax.ppermute(value, "dp", [(i, (i + step) % size) for i in range(size)])


def gather_blocks(rows):
    half = rows.shape[1] // 2
    behind_two, ahead_two = shift(rows, 2), shift(rows, -2)
    behind_one, ahead_one = shift(rows, 1), shift(rows, -1)
    behind_three, ahead_three = shift(behind_two, 1), shift(ahead_two, -1)
    away = jnp.concatenate(
        [shift(behind_two[:, :half], 2), shift(ahead_two[:, half:], -2)], axis=1
    )
    return jnp.concatenate(
        [rows, behind_one, ahead_one, behind_two, ahead_two, behind_three, ahead_three, away], axis=0
    )


def reduce_blocks(partial, rows):
    half = partial.shape[1] // 2
    block = [partial[i * rows : (i + 1) * rows] for i in range(8)]
    own, behind_one, ahead_one, behind_two, ahead_two, behind_three, ahead_three, away = block
    send = lambda value, step: shift(value.astype(jnp.bfloat16), step).astype(jnp.float32)
    down, up = send(behind_three, -1), send(ahead_three, 1)
    away_down, away_up = send(away[:, :half], -2), send(away[:, half:], 2)
    near = send(behind_one, -1) + send(ahead_one, 1)
    down, up = down + behind_two, up + ahead_two
    down = jnp.concatenate([down[:, :half] + away_down, down[:, half:]], axis=1)
    up = jnp.concatenate([up[:, :half], up[:, half:] + away_up], axis=1)
    return own + near + (send(down, -2) + send(up, 2))


def swap(value):
    return lax.all_to_all(value, ("tok", "expert"), split_axis=0, concat_axis=0, tiled=True)


def sum_everywhere(part):
    slots, width = part.shape
    mine = jnp.sum(swap(part), axis=0, keepdims=True)
    copies = jnp.broadcast_to(mine, (lax.axis_size("dp"), width))
    seen = lax.all_to_all(copies, "dp", split_axis=0, concat_axis=0, tiled=True)
    return swap(jnp.broadcast_to(jnp.sum(seen, axis=0, keepdims=True), (slots, width)))


def body(tokens, router, expert_in, expert_out, grad_out):
    patches, image_grad = tokens[0], grad_out[0]
    model_width = patches.shape[1]
    router_scores = jnp.dot(patches, router, preferred_element_type=jnp.float32)
    combine = jax.nn.softmax(router_scores, axis=1)
    combine_rounded = combine.astype(jnp.bfloat16)
    stored_residuals = forward_iterates(router_scores)
    assignment_matrix = jnp.exp(stored_residuals[-1][1])
    dispatch_rounded = assignment_matrix.astype(jnp.bfloat16)
    slot_part = jnp.dot(dispatch_rounded.T, patches, preferred_element_type=jnp.float32).astype(
        jnp.bfloat16
    )
    grad_part = jnp.dot(combine_rounded.T, image_grad, preferred_element_type=jnp.float32).astype(
        jnp.bfloat16
    )
    rows = swap(jnp.concatenate([slot_part, grad_part], axis=1))
    gathered = gather_blocks(rows)
    all_in, all_grad = gathered[:, :model_width], gathered[:, model_width:]
    weight_in = expert_in[0]
    weight_out = expert_out[0]
    hidden_pre = jnp.dot(all_in, weight_in, preferred_element_type=jnp.float32)
    activated, derivative = gelu_pair(hidden_pre)
    hidden_act = activated.astype(jnp.bfloat16)
    grad_act = lax.dot_general(
        all_grad, weight_out, (((1,), (1,)), ((), ())), preferred_element_type=jnp.float32
    )
    grad_pre = (grad_act * derivative).astype(jnp.bfloat16)
    forward_rows = jnp.dot(hidden_act, weight_out, preferred_element_type=jnp.float32)
    backward_rows = lax.dot_general(
        grad_pre, weight_in, (((1,), (1,)), ((), ())), preferred_element_type=jnp.float32
    )
    summed = reduce_blocks(
        jnp.concatenate([forward_rows, backward_rows], axis=1), rows.shape[0]
    ).astype(jnp.bfloat16)
    grad_win = lax.dot_general(
        all_in, grad_pre, (((0,), (0,)), ((), ())), preferred_element_type=jnp.float32
    ).astype(jnp.bfloat16)[None]
    out_weight_gradient = lax.dot_general(
        hidden_act, all_grad, (((0,), (0,)), ((), ())), preferred_element_type=jnp.float32
    ).astype(jnp.bfloat16)[None]
    back = swap(summed)
    back_out, back_grad = back[:, :model_width], back[:, model_width:]
    grad_comb = lax.dot_general(
        image_grad, back_out, (((1,), (1,)), ((), ())), preferred_element_type=jnp.float32
    )
    logit_cotangent = combine * (grad_comb - jnp.sum(combine * grad_comb, axis=1, keepdims=True))
    doubly_stochastic_adjoint = (
        lax.dot_general(
            patches, back_grad, (((1,), (1,)), ((), ())), preferred_element_type=jnp.float32
        )
        * assignment_matrix
    )
    doubly_stochastic_adjoint = backward_sequence(doubly_stochastic_adjoint, stored_residuals)
    accumulated_cotangent = (logit_cotangent + doubly_stochastic_adjoint).astype(jnp.bfloat16)
    router_part = lax.dot_general(
        accumulated_cotangent, patches, (((0,), (0,)), ((), ())), preferred_element_type=jnp.float32
    )
    grad_router = sum_everywhere(router_part).T
    grad_tokens = (
        jnp.dot(dispatch_rounded, back_grad, preferred_element_type=jnp.float32)
        + lax.dot_general(
            accumulated_cotangent, router, (((1,), (1,)), ((), ())), preferred_element_type=jnp.float32
        )
    ).astype(jnp.bfloat16)[None]
    return (grad_tokens, grad_router, grad_win, out_weight_gradient)


def solution(mesh):
    return jax.shard_map(
        body,
        mesh=mesh,
        in_specs=(
            P(("dp", "tok", "expert"), None, None),
            P(),
            P(("tok", "expert"), None, "dp"),
            P(("tok", "expert"), "dp", None),
            P(("dp", "tok", "expert"), None, None),
        ),
        out_specs=(
            P(("dp", "tok", "expert"), None, None),
            P(),
            P(("tok", "expert"), None, "dp"),
            P(("tok", "expert"), "dp", None),
        ),
        check_vma=False,
    )
```

```python
import jax
import jax.numpy as jnp
from jax import lax
from jax.sharding import PartitionSpec as P

ITERS = 4


GELU_SCALE = 0.7978845608028654
GELU_CUBIC = 0.044715


def gelu_pair(hidden_pre):
    inner_arg = GELU_SCALE * (hidden_pre + GELU_CUBIC * hidden_pre * hidden_pre * hidden_pre)
    tanh_val = jnp.tanh(inner_arg)
    activated = 0.5 * hidden_pre * (1.0 + tanh_val)
    derivative = 0.5 * (1.0 + tanh_val) + 0.5 * hidden_pre * (
        1.0 - tanh_val * tanh_val
    ) * GELU_SCALE * (1.0 + 3.0 * GELU_CUBIC * hidden_pre * hidden_pre)
    return (activated, derivative)


def forward_iterates(router_scores):
    iterate = router_scores
    stored_residuals = []
    for sweep_index in range(ITERS):
        line_divisor_factor = iterate - jax.nn.logsumexp(iterate, axis=1, keepdims=True)
        column_divisor = line_divisor_factor - jax.nn.logsumexp(
            line_divisor_factor, axis=0, keepdims=True
        )
        stored_residuals.append((line_divisor_factor, column_divisor))
        iterate = column_divisor
    return stored_residuals


def backward_sequence(gradient, stored_residuals):
    for line_divisor_factor, column_divisor in reversed(stored_residuals):
        gradient = gradient - jnp.exp(column_divisor) * jnp.sum(gradient, axis=0, keepdims=True)
        gradient = gradient - jnp.exp(line_divisor_factor) * jnp.sum(
            gradient, axis=1, keepdims=True
        )
    return gradient


def shift(value, step):
    size = lax.axis_size("dp")
    return lax.ppermute(value, "dp", [(i, (i + step) % size) for i in range(size)])


def swap(value):
    return lax.all_to_all(value, ("tok", "expert"), split_axis=0, concat_axis=0, tiled=True)


def sum_everywhere(part):
    slots, width = part.shape
    mine = jnp.sum(swap(part), axis=0, keepdims=True)
    copies = jnp.broadcast_to(mine, (lax.axis_size("dp"), width))
    seen = lax.all_to_all(copies, "dp", split_axis=0, concat_axis=0, tiled=True)
    return swap(jnp.broadcast_to(jnp.sum(seen, axis=0, keepdims=True), (slots, width)))


def paired_swap(first, second):
    moved = swap(jnp.stack([first, second], axis=1))
    return jnp.concatenate([moved[:, 0], moved[:, 1]], axis=1)


def expert_rows(rows, weight_in, weight_out):
    width = weight_in.shape[0]
    row_in, row_grad = rows[:, :width], rows[:, width:]
    hidden_pre = jnp.dot(row_in, weight_in, preferred_element_type=jnp.float32)
    activated, derivative = gelu_pair(hidden_pre)
    hidden_act = activated.astype(jnp.bfloat16)
    grad_act = lax.dot_general(
        row_grad, weight_out, (((1,), (1,)), ((), ())), preferred_element_type=jnp.float32
    )
    grad_pre = (grad_act * derivative).astype(jnp.bfloat16)
    forward_rows = jnp.dot(hidden_act, weight_out, preferred_element_type=jnp.float32)
    backward_rows = lax.dot_general(
        grad_pre, weight_in, (((1,), (1,)), ((), ())), preferred_element_type=jnp.float32
    )
    return hidden_act, grad_pre, forward_rows, backward_rows


def body(tokens, router, expert_in, expert_out, grad_out):
    patches, image_grad = tokens[0], grad_out[0]
    model_width = patches.shape[1]
    router_scores = jnp.dot(patches, router, preferred_element_type=jnp.float32)
    combine = jax.nn.softmax(router_scores, axis=1)
    combine_rounded = combine.astype(jnp.bfloat16)
    stored_residuals = forward_iterates(router_scores)
    assignment_matrix = jnp.exp(stored_residuals[-1][1])
    dispatch_rounded = assignment_matrix.astype(jnp.bfloat16)
    slot_part = jnp.dot(dispatch_rounded.T, patches, preferred_element_type=jnp.float32).astype(
        jnp.bfloat16
    )
    grad_part = jnp.dot(combine_rounded.T, image_grad, preferred_element_type=jnp.float32).astype(
        jnp.bfloat16
    )
    rows = paired_swap(slot_part, grad_part)
    weight_in = expert_in[0]
    weight_out = expert_out[0]
    count, half = rows.shape[0], model_width

    behind_two, ahead_two = shift(rows, 2), shift(rows, -2)
    behind_one, ahead_one = shift(rows, 1), shift(rows, -1)
    behind_three, ahead_three = shift(behind_two, 1), shift(ahead_two, -1)
    away = jnp.concatenate(
        [shift(behind_two[:, :half], 2), shift(ahead_two[:, half:], -2)], axis=1
    )
    near_rows = jnp.concatenate([rows, behind_one, ahead_one, behind_two, ahead_two], axis=0)
    far_rows = jnp.concatenate([behind_three, ahead_three, away], axis=0)
    near_act, near_pre, near_forward, near_backward = expert_rows(near_rows, weight_in, weight_out)

    def block(forward_rows, backward_rows, place):
        piece = slice(place * count, (place + 1) * count)
        return jnp.concatenate([forward_rows[piece], backward_rows[piece]], axis=1)

    send = lambda value, step: shift(value.astype(jnp.bfloat16), step).astype(jnp.float32)
    own = block(near_forward, near_backward, 0)
    to_behind, to_ahead, far_rows = lax.optimization_barrier(
        (
            block(near_forward, near_backward, 1).astype(jnp.bfloat16),
            block(near_forward, near_backward, 2).astype(jnp.bfloat16),
            far_rows,
        )
    )
    near = send(to_behind, -1) + send(to_ahead, 1)
    far_act, far_pre, far_forward, far_backward = expert_rows(far_rows, weight_in, weight_out)
    down = send(block(far_forward, far_backward, 0), -1)
    up = send(block(far_forward, far_backward, 1), 1)
    away_down, away_up = send(far_forward[2 * count :], -2), send(far_backward[2 * count :], 2)
    down = down + block(near_forward, near_backward, 3)
    up = up + block(near_forward, near_backward, 4)
    down = jnp.concatenate([down[:, :half] + away_down, down[:, half:]], axis=1)
    up = jnp.concatenate([up[:, :half], up[:, half:] + away_up], axis=1)
    summed = (own + near + (send(down, -2) + send(up, 2))).astype(jnp.bfloat16)

    all_rows = jnp.concatenate([near_rows, far_rows], axis=0)
    grad_pre = jnp.concatenate([near_pre, far_pre], axis=0)
    hidden_act = jnp.concatenate([near_act, far_act], axis=0)
    grad_win = lax.dot_general(
        all_rows[:, :half], grad_pre, (((0,), (0,)), ((), ())), preferred_element_type=jnp.float32
    ).astype(jnp.bfloat16)[None]
    out_weight_gradient = lax.dot_general(
        hidden_act, all_rows[:, half:], (((0,), (0,)), ((), ())), preferred_element_type=jnp.float32
    ).astype(jnp.bfloat16)[None]
    back = paired_swap(summed[:, :half], summed[:, half:])
    back_out, back_grad = back[:, :half], back[:, half:]
    grad_comb = lax.dot_general(
        image_grad, back_out, (((1,), (1,)), ((), ())), preferred_element_type=jnp.float32
    )
    logit_cotangent = combine * (grad_comb - jnp.sum(combine * grad_comb, axis=1, keepdims=True))
    doubly_stochastic_adjoint = (
        lax.dot_general(
            patches, back_grad, (((1,), (1,)), ((), ())), preferred_element_type=jnp.float32
        )
        * assignment_matrix
    )
    doubly_stochastic_adjoint = backward_sequence(doubly_stochastic_adjoint, stored_residuals)
    accumulated_cotangent = (logit_cotangent + doubly_stochastic_adjoint).astype(jnp.bfloat16)
    router_part = lax.dot_general(
        accumulated_cotangent, patches, (((0,), (0,)), ((), ())), preferred_element_type=jnp.float32
    )
    grad_router = sum_everywhere(router_part).T
    grad_tokens = (
        jnp.dot(dispatch_rounded, back_grad, preferred_element_type=jnp.float32)
        + lax.dot_general(
            accumulated_cotangent, router, (((1,), (1,)), ((), ())), preferred_element_type=jnp.float32
        )
    ).astype(jnp.bfloat16)[None]
    return (grad_tokens, grad_router, grad_win, out_weight_gradient)


def solution(mesh):
    return jax.shard_map(
        body,
        mesh=mesh,
        in_specs=(
            P(("dp", "tok", "expert"), None, None),
            P(),
            P(("tok", "expert"), None, "dp"),
            P(("tok", "expert"), "dp", None),
            P(("dp", "tok", "expert"), None, None),
        ),
        out_specs=(
            P(("dp", "tok", "expert"), None, None),
            P(),
            P(("tok", "expert"), None, "dp"),
            P(("tok", "expert"), "dp", None),
        ),
        check_vma=False,
    )
```

```python
import jax
import jax.numpy as jnp
from jax import lax
from jax.sharding import PartitionSpec as P

ITERS = 4


GELU_SCALE = 0.7978845608028654
GELU_CUBIC = 0.044715


def gelu_pair(hidden_pre):
    inner_arg = GELU_SCALE * (hidden_pre + GELU_CUBIC * hidden_pre * hidden_pre * hidden_pre)
    tanh_val = jnp.tanh(inner_arg)
    activated = 0.5 * hidden_pre * (1.0 + tanh_val)
    derivative = 0.5 * (1.0 + tanh_val) + 0.5 * hidden_pre * (
        1.0 - tanh_val * tanh_val
    ) * GELU_SCALE * (1.0 + 3.0 * GELU_CUBIC * hidden_pre * hidden_pre)
    return (activated, derivative)


def forward_iterates(router_scores):
    iterate = router_scores
    stored_residuals = []
    for sweep_index in range(ITERS):
        line_divisor_factor = iterate - jax.nn.logsumexp(iterate, axis=1, keepdims=True)
        column_divisor = line_divisor_factor - jax.nn.logsumexp(
            line_divisor_factor, axis=0, keepdims=True
        )
        stored_residuals.append((line_divisor_factor, column_divisor))
        iterate = column_divisor
    return stored_residuals


def backward_sequence(gradient, stored_residuals):
    for line_divisor_factor, column_divisor in reversed(stored_residuals):
        gradient = gradient - jnp.exp(column_divisor) * jnp.sum(gradient, axis=0, keepdims=True)
        gradient = gradient - jnp.exp(line_divisor_factor) * jnp.sum(
            gradient, axis=1, keepdims=True
        )
    return gradient


def shift(value, step):
    size = lax.axis_size("dp")
    return lax.ppermute(value, "dp", [(i, (i + step) % size) for i in range(size)])


def gather_blocks(rows):
    half = rows.shape[1] // 2
    behind_two, ahead_two = shift(rows, 2), shift(rows, -2)
    behind_one, ahead_one = shift(rows, 1), shift(rows, -1)
    behind_three, ahead_three = shift(behind_two, 1), shift(ahead_two, -1)
    away = jnp.concatenate(
        [shift(behind_two[:, :half], 2), shift(ahead_two[:, half:], -2)], axis=1
    )
    return jnp.concatenate(
        [rows, behind_one, ahead_one, behind_two, ahead_two, behind_three, ahead_three, away], axis=0
    )


def reduce_blocks(partial, rows):
    half = partial.shape[1] // 2
    block = [partial[i * rows : (i + 1) * rows] for i in range(8)]
    own, behind_one, ahead_one, behind_two, ahead_two, behind_three, ahead_three, away = block
    send = lambda value, step: shift(value.astype(jnp.bfloat16), step).astype(jnp.float32)
    down, up = send(behind_three, -1), send(ahead_three, 1)
    away_down, away_up = send(away[:, :half], -2), send(away[:, half:], 2)
    near = send(behind_one, -1) + send(ahead_one, 1)
    down, up = down + behind_two, up + ahead_two
    down = jnp.concatenate([down[:, :half] + away_down, down[:, half:]], axis=1)
    up = jnp.concatenate([up[:, :half], up[:, half:] + away_up], axis=1)
    return own + near + (send(down, -2) + send(up, 2))


def swap(value):
    return lax.all_to_all(value, ("tok", "expert"), split_axis=0, concat_axis=0, tiled=True)


def sum_everywhere(part):
    slots, width = part.shape
    mine = jnp.sum(swap(part), axis=0, keepdims=True)
    copies = jnp.broadcast_to(mine, (lax.axis_size("dp"), width))
    seen = lax.all_to_all(copies, "dp", split_axis=0, concat_axis=0, tiled=True)
    return swap(jnp.broadcast_to(jnp.sum(seen, axis=0, keepdims=True), (slots, width)))


def paired_swap(first, second):
    moved = swap(jnp.stack([first, second], axis=1))
    return jnp.concatenate([moved[:, 0], moved[:, 1]], axis=1)


def body(tokens, router, expert_in, expert_out, grad_out):
    patches, image_grad = tokens[0], grad_out[0]
    model_width = patches.shape[1]
    router_scores = jnp.dot(patches, router, preferred_element_type=jnp.float32)
    combine = jax.nn.softmax(router_scores, axis=1)
    combine_rounded = combine.astype(jnp.bfloat16)
    stored_residuals = forward_iterates(router_scores)
    assignment_matrix = jnp.exp(stored_residuals[-1][1])
    dispatch_rounded = assignment_matrix.astype(jnp.bfloat16)
    slot_part = jnp.dot(dispatch_rounded.T, patches, preferred_element_type=jnp.float32).astype(
        jnp.bfloat16
    )
    grad_part = jnp.dot(combine_rounded.T, image_grad, preferred_element_type=jnp.float32).astype(
        jnp.bfloat16
    )
    rows = paired_swap(slot_part, grad_part)
    gathered = gather_blocks(rows)
    all_in, all_grad = gathered[:, :model_width], gathered[:, model_width:]
    weight_in = expert_in[0]
    weight_out = expert_out[0]
    hidden_pre = jnp.dot(all_in, weight_in, preferred_element_type=jnp.float32)
    activated, derivative = gelu_pair(hidden_pre)
    hidden_act = activated.astype(jnp.bfloat16)
    grad_act = lax.dot_general(
        all_grad, weight_out, (((1,), (1,)), ((), ())), preferred_element_type=jnp.float32
    )
    grad_pre = (grad_act * derivative).astype(jnp.bfloat16)
    forward_rows = jnp.dot(hidden_act, weight_out, preferred_element_type=jnp.float32)
    backward_rows = lax.dot_general(
        grad_pre, weight_in, (((1,), (1,)), ((), ())), preferred_element_type=jnp.float32
    )
    summed = reduce_blocks(
        jnp.concatenate([forward_rows, backward_rows], axis=1), rows.shape[0]
    ).astype(jnp.bfloat16)
    grad_win = lax.dot_general(
        all_in, grad_pre, (((0,), (0,)), ((), ())), preferred_element_type=jnp.float32
    ).astype(jnp.bfloat16)[None]
    out_weight_gradient = lax.dot_general(
        hidden_act, all_grad, (((0,), (0,)), ((), ())), preferred_element_type=jnp.float32
    ).astype(jnp.bfloat16)[None]
    back = paired_swap(summed[:, :model_width], summed[:, model_width:])
    back_out, back_grad = back[:, :model_width], back[:, model_width:]
    grad_comb = lax.dot_general(
        image_grad, back_out, (((1,), (1,)), ((), ())), preferred_element_type=jnp.float32
    )
    logit_cotangent = combine * (grad_comb - jnp.sum(combine * grad_comb, axis=1, keepdims=True))
    doubly_stochastic_adjoint = (
        lax.dot_general(
            patches, back_grad, (((1,), (1,)), ((), ())), preferred_element_type=jnp.float32
        )
        * assignment_matrix
    )
    doubly_stochastic_adjoint = backward_sequence(doubly_stochastic_adjoint, stored_residuals)
    accumulated_cotangent = (logit_cotangent + doubly_stochastic_adjoint).astype(jnp.bfloat16)
    router_part = lax.dot_general(
        accumulated_cotangent, patches, (((0,), (0,)), ((), ())), preferred_element_type=jnp.float32
    )
    grad_router = sum_everywhere(router_part).T
    grad_tokens = (
        jnp.dot(dispatch_rounded, back_grad, preferred_element_type=jnp.float32)
        + lax.dot_general(
            accumulated_cotangent, router, (((1,), (1,)), ((), ())), preferred_element_type=jnp.float32
        )
    ).astype(jnp.bfloat16)[None]
    return (grad_tokens, grad_router, grad_win, out_weight_gradient)


def solution(mesh):
    return jax.shard_map(
        body,
        mesh=mesh,
        in_specs=(
            P(("dp", "tok", "expert"), None, None),
            P(),
            P(("tok", "expert"), None, "dp"),
            P(("tok", "expert"), "dp", None),
            P(("dp", "tok", "expert"), None, None),
        ),
        out_specs=(
            P(("dp", "tok", "expert"), None, None),
            P(),
            P(("tok", "expert"), None, "dp"),
            P(("tok", "expert"), "dp", None),
        ),
        check_vma=False,
    )
```

```python
import jax
import jax.numpy as jnp
from jax import lax
from jax.sharding import PartitionSpec as P

ITERS = 4


GELU_SCALE = 0.7978845608028654
GELU_CUBIC = 0.044715


def gelu_pair(hidden_pre):
    inner_arg = GELU_SCALE * (hidden_pre + GELU_CUBIC * hidden_pre * hidden_pre * hidden_pre)
    tanh_val = jnp.tanh(inner_arg)
    activated = 0.5 * hidden_pre * (1.0 + tanh_val)
    derivative = 0.5 * (1.0 + tanh_val) + 0.5 * hidden_pre * (
        1.0 - tanh_val * tanh_val
    ) * GELU_SCALE * (1.0 + 3.0 * GELU_CUBIC * hidden_pre * hidden_pre)
    return (activated, derivative)


def forward_iterates(router_scores):
    iterate = router_scores
    stored_residuals = []
    for sweep_index in range(ITERS):
        line_divisor_factor = iterate - jax.nn.logsumexp(iterate, axis=1, keepdims=True)
        column_divisor = line_divisor_factor - jax.nn.logsumexp(
            line_divisor_factor, axis=0, keepdims=True
        )
        stored_residuals.append((line_divisor_factor, column_divisor))
        iterate = column_divisor
    return stored_residuals


def backward_sequence(gradient, stored_residuals):
    for line_divisor_factor, column_divisor in reversed(stored_residuals):
        gradient = gradient - jnp.exp(column_divisor) * jnp.sum(gradient, axis=0, keepdims=True)
        gradient = gradient - jnp.exp(line_divisor_factor) * jnp.sum(
            gradient, axis=1, keepdims=True
        )
    return gradient


def shift(value, step):
    size = lax.axis_size("dp")
    return lax.ppermute(value, "dp", [(i, (i + step) % size) for i in range(size)])


def gather_blocks(rows):
    half = rows.shape[1] // 2
    behind_two, ahead_two = shift(rows, 2), shift(rows, -2)
    behind_one, ahead_one = shift(rows, 1), shift(rows, -1)
    behind_three, ahead_three = shift(behind_two, 1), shift(ahead_two, -1)
    away = jnp.concatenate(
        [shift(behind_two[:, :half], 2), shift(ahead_two[:, half:], -2)], axis=1
    )
    return jnp.concatenate(
        [rows, behind_one, ahead_one, behind_two, ahead_two, behind_three, ahead_three, away], axis=0
    )


def reduce_blocks(partial, rows):
    half = partial.shape[1] // 2
    block = [partial[i * rows : (i + 1) * rows] for i in range(8)]
    own, behind_one, ahead_one, behind_two, ahead_two, behind_three, ahead_three, away = block
    narrow = jnp.bfloat16
    send = lambda value, step: shift(value.astype(narrow), step).astype(jnp.float32)
    down, up = shift(behind_three.astype(narrow), -1), shift(ahead_three.astype(narrow), 1)
    away_down, away_up = send(away[:, :half], -2), send(away[:, half:], 2)
    down, up, to_behind, to_ahead = lax.optimization_barrier(
        (down, up, behind_one.astype(narrow), ahead_one.astype(narrow))
    )
    near = send(to_behind, -1) + send(to_ahead, 1)
    down, up = down.astype(jnp.float32), up.astype(jnp.float32)
    down, up = down + behind_two, up + ahead_two
    down = jnp.concatenate([down[:, :half] + away_down, down[:, half:]], axis=1)
    up = jnp.concatenate([up[:, :half], up[:, half:] + away_up], axis=1)
    return own + near + (send(down, -2) + send(up, 2))


def swap(value):
    return lax.all_to_all(value, ("tok", "expert"), split_axis=0, concat_axis=0, tiled=True)


def sum_everywhere(part):
    slots, width = part.shape
    mine = jnp.sum(swap(part), axis=0, keepdims=True)
    copies = jnp.broadcast_to(mine, (lax.axis_size("dp"), width))
    seen = lax.all_to_all(copies, "dp", split_axis=0, concat_axis=0, tiled=True)
    return swap(jnp.broadcast_to(jnp.sum(seen, axis=0, keepdims=True), (slots, width)))


def paired_swap(first, second):
    moved = swap(jnp.stack([first, second], axis=1))
    return jnp.concatenate([moved[:, 0], moved[:, 1]], axis=1)


def body(tokens, router, expert_in, expert_out, grad_out):
    patches, image_grad = tokens[0], grad_out[0]
    model_width = patches.shape[1]
    router_scores = jnp.dot(patches, router, preferred_element_type=jnp.float32)
    combine = jax.nn.softmax(router_scores, axis=1)
    combine_rounded = combine.astype(jnp.bfloat16)
    stored_residuals = forward_iterates(router_scores)
    assignment_matrix = jnp.exp(stored_residuals[-1][1])
    dispatch_rounded = assignment_matrix.astype(jnp.bfloat16)
    slot_part = jnp.dot(dispatch_rounded.T, patches, preferred_element_type=jnp.float32).astype(
        jnp.bfloat16
    )
    grad_part = jnp.dot(combine_rounded.T, image_grad, preferred_element_type=jnp.float32).astype(
        jnp.bfloat16
    )
    rows = paired_swap(slot_part, grad_part)
    gathered = gather_blocks(rows)
    all_in, all_grad = gathered[:, :model_width], gathered[:, model_width:]
    weight_in = expert_in[0]
    weight_out = expert_out[0]
    hidden_pre = jnp.dot(all_in, weight_in, preferred_element_type=jnp.float32)
    activated, derivative = gelu_pair(hidden_pre)
    hidden_act = activated.astype(jnp.bfloat16)
    grad_act = lax.dot_general(
        all_grad, weight_out, (((1,), (1,)), ((), ())), preferred_element_type=jnp.float32
    )
    grad_pre = (grad_act * derivative).astype(jnp.bfloat16)
    forward_rows = jnp.dot(hidden_act, weight_out, preferred_element_type=jnp.float32)
    backward_rows = lax.dot_general(
        grad_pre, weight_in, (((1,), (1,)), ((), ())), preferred_element_type=jnp.float32
    )
    summed = reduce_blocks(
        jnp.concatenate([forward_rows, backward_rows], axis=1), rows.shape[0]
    ).astype(jnp.bfloat16)
    grad_win = lax.dot_general(
        all_in, grad_pre, (((0,), (0,)), ((), ())), preferred_element_type=jnp.float32
    ).astype(jnp.bfloat16)[None]
    out_weight_gradient = lax.dot_general(
        hidden_act, all_grad, (((0,), (0,)), ((), ())), preferred_element_type=jnp.float32
    ).astype(jnp.bfloat16)[None]
    back = paired_swap(summed[:, :model_width], summed[:, model_width:])
    back_out, back_grad = back[:, :model_width], back[:, model_width:]
    grad_comb = lax.dot_general(
        image_grad, back_out, (((1,), (1,)), ((), ())), preferred_element_type=jnp.float32
    )
    logit_cotangent = combine * (grad_comb - jnp.sum(combine * grad_comb, axis=1, keepdims=True))
    doubly_stochastic_adjoint = (
        lax.dot_general(
            patches, back_grad, (((1,), (1,)), ((), ())), preferred_element_type=jnp.float32
        )
        * assignment_matrix
    )
    doubly_stochastic_adjoint = backward_sequence(doubly_stochastic_adjoint, stored_residuals)
    accumulated_cotangent = (logit_cotangent + doubly_stochastic_adjoint).astype(jnp.bfloat16)
    router_part = lax.dot_general(
        accumulated_cotangent, patches, (((0,), (0,)), ((), ())), preferred_element_type=jnp.float32
    )
    grad_router = sum_everywhere(router_part).T
    grad_tokens = (
        jnp.dot(dispatch_rounded, back_grad, preferred_element_type=jnp.float32)
        + lax.dot_general(
            accumulated_cotangent, router, (((1,), (1,)), ((), ())), preferred_element_type=jnp.float32
        )
    ).astype(jnp.bfloat16)[None]
    return (grad_tokens, grad_router, grad_win, out_weight_gradient)


def solution(mesh):
    return jax.shard_map(
        body,
        mesh=mesh,
        in_specs=(
            P(("dp", "tok", "expert"), None, None),
            P(),
            P(("tok", "expert"), None, "dp"),
            P(("tok", "expert"), "dp", None),
            P(("dp", "tok", "expert"), None, None),
        ),
        out_specs=(
            P(("dp", "tok", "expert"), None, None),
            P(),
            P(("tok", "expert"), None, "dp"),
            P(("tok", "expert"), "dp", None),
        ),
        check_vma=False,
    )
```

```python
import jax
import jax.numpy as jnp
from jax import lax
from jax.sharding import PartitionSpec as P

ITERS = 4


GELU_SCALE = 0.7978845608028654
GELU_CUBIC = 0.044715


def gelu_pair(hidden_pre):
    inner_arg = GELU_SCALE * (hidden_pre + GELU_CUBIC * hidden_pre * hidden_pre * hidden_pre)
    tanh_val = jnp.tanh(inner_arg)
    activated = 0.5 * hidden_pre * (1.0 + tanh_val)
    derivative = 0.5 * (1.0 + tanh_val) + 0.5 * hidden_pre * (
        1.0 - tanh_val * tanh_val
    ) * GELU_SCALE * (1.0 + 3.0 * GELU_CUBIC * hidden_pre * hidden_pre)
    return (activated, derivative)


def forward_iterates(router_scores):
    iterate = router_scores
    stored_residuals = []
    for sweep_index in range(ITERS):
        line_divisor_factor = iterate - jax.nn.logsumexp(iterate, axis=1, keepdims=True)
        column_divisor = line_divisor_factor - jax.nn.logsumexp(
            line_divisor_factor, axis=0, keepdims=True
        )
        stored_residuals.append((line_divisor_factor, column_divisor))
        iterate = column_divisor
    return stored_residuals


def backward_sequence(gradient, stored_residuals):
    for line_divisor_factor, column_divisor in reversed(stored_residuals):
        gradient = gradient - jnp.exp(column_divisor) * jnp.sum(gradient, axis=0, keepdims=True)
        gradient = gradient - jnp.exp(line_divisor_factor) * jnp.sum(
            gradient, axis=1, keepdims=True
        )
    return gradient


def shift(value, step):
    size = lax.axis_size("dp")
    return lax.ppermute(value, "dp", [(i, (i + step) % size) for i in range(size)])


def shift_two(value):
    size = lax.axis_size("dp")
    pairs = [(i, (i + (2 if i % 2 == 0 else -2)) % size) for i in range(size)]
    return lax.ppermute(value, "dp", pairs)


def is_even():
    return lax.axis_index("dp") % 2 == 0


def gather_blocks(rows):
    behind_two, ahead_two = shift(rows, 2), shift(rows, -2)
    behind = shift(jnp.concatenate([rows, behind_two], axis=0), 1)
    ahead = shift(jnp.concatenate([rows, ahead_two], axis=0), -1)
    away = shift_two(jnp.where(is_even(), behind_two, ahead_two))
    return jnp.concatenate([rows, behind, ahead, behind_two, ahead_two, away], axis=0)


def reduce_blocks(partial, rows):
    wide = jnp.float32
    narrow = partial.astype(jnp.bfloat16)
    own = partial[:rows]
    down, up = shift(narrow[rows : 3 * rows], -1), shift(narrow[3 * rows : 5 * rows], 1)
    away = shift_two(narrow[7 * rows :]).astype(wide)
    near = down[:rows].astype(wide) + up[:rows].astype(wide)
    nothing = jnp.zeros_like(away)
    down_sum = partial[5 * rows : 6 * rows] + down[rows:].astype(wide)
    up_sum = partial[6 * rows : 7 * rows] + up[rows:].astype(wide)
    up_sum = up_sum + jnp.where(is_even(), away, nothing)
    down_sum = down_sum + jnp.where(is_even(), nothing, away)
    return (
        own
        + near
        + shift(down_sum.astype(jnp.bfloat16), -2).astype(wide)
        + shift(up_sum.astype(jnp.bfloat16), 2).astype(wide)
    )


def swap(value):
    return lax.all_to_all(value, ("tok", "expert"), split_axis=0, concat_axis=0, tiled=True)


def sum_everywhere(part):
    slots, width = part.shape
    mine = jnp.sum(swap(part), axis=0, keepdims=True)
    copies = jnp.broadcast_to(mine, (lax.axis_size("dp"), width))
    seen = lax.all_to_all(copies, "dp", split_axis=0, concat_axis=0, tiled=True)
    return swap(jnp.broadcast_to(jnp.sum(seen, axis=0, keepdims=True), (slots, width)))


def paired_swap(first, second):
    moved = swap(jnp.stack([first, second], axis=1))
    return jnp.concatenate([moved[:, 0], moved[:, 1]], axis=1)


def body(tokens, router, expert_in, expert_out, grad_out):
    patches, image_grad = tokens[0], grad_out[0]
    model_width = patches.shape[1]
    router_scores = jnp.dot(patches, router, preferred_element_type=jnp.float32)
    combine = jax.nn.softmax(router_scores, axis=1)
    combine_rounded = combine.astype(jnp.bfloat16)
    stored_residuals = forward_iterates(router_scores)
    assignment_matrix = jnp.exp(stored_residuals[-1][1])
    dispatch_rounded = assignment_matrix.astype(jnp.bfloat16)
    slot_part = jnp.dot(dispatch_rounded.T, patches, preferred_element_type=jnp.float32).astype(
        jnp.bfloat16
    )
    grad_part = jnp.dot(combine_rounded.T, image_grad, preferred_element_type=jnp.float32).astype(
        jnp.bfloat16
    )
    rows = paired_swap(slot_part, grad_part)
    gathered = gather_blocks(rows)
    all_in, all_grad = gathered[:, :model_width], gathered[:, model_width:]
    weight_in = expert_in[0]
    weight_out = expert_out[0]
    hidden_pre = jnp.dot(all_in, weight_in, preferred_element_type=jnp.float32)
    activated, derivative = gelu_pair(hidden_pre)
    hidden_act = activated.astype(jnp.bfloat16)
    grad_act = lax.dot_general(
        all_grad, weight_out, (((1,), (1,)), ((), ())), preferred_element_type=jnp.float32
    )
    grad_pre = (grad_act * derivative).astype(jnp.bfloat16)
    forward_rows = jnp.dot(hidden_act, weight_out, preferred_element_type=jnp.float32)
    backward_rows = lax.dot_general(
        grad_pre, weight_in, (((1,), (1,)), ((), ())), preferred_element_type=jnp.float32
    )
    summed = reduce_blocks(
        jnp.concatenate([forward_rows, backward_rows], axis=1), rows.shape[0]
    ).astype(jnp.bfloat16)
    grad_win = lax.dot_general(
        all_in, grad_pre, (((0,), (0,)), ((), ())), preferred_element_type=jnp.float32
    ).astype(jnp.bfloat16)[None]
    out_weight_gradient = lax.dot_general(
        hidden_act, all_grad, (((0,), (0,)), ((), ())), preferred_element_type=jnp.float32
    ).astype(jnp.bfloat16)[None]
    back = paired_swap(summed[:, :model_width], summed[:, model_width:])
    back_out, back_grad = back[:, :model_width], back[:, model_width:]
    grad_comb = lax.dot_general(
        image_grad, back_out, (((1,), (1,)), ((), ())), preferred_element_type=jnp.float32
    )
    logit_cotangent = combine * (grad_comb - jnp.sum(combine * grad_comb, axis=1, keepdims=True))
    doubly_stochastic_adjoint = (
        lax.dot_general(
            patches, back_grad, (((1,), (1,)), ((), ())), preferred_element_type=jnp.float32
        )
        * assignment_matrix
    )
    doubly_stochastic_adjoint = backward_sequence(doubly_stochastic_adjoint, stored_residuals)
    accumulated_cotangent = (logit_cotangent + doubly_stochastic_adjoint).astype(jnp.bfloat16)
    router_part = lax.dot_general(
        accumulated_cotangent, patches, (((0,), (0,)), ((), ())), preferred_element_type=jnp.float32
    )
    grad_router = sum_everywhere(router_part).T
    grad_tokens = (
        jnp.dot(dispatch_rounded, back_grad, preferred_element_type=jnp.float32)
        + lax.dot_general(
            accumulated_cotangent, router, (((1,), (1,)), ((), ())), preferred_element_type=jnp.float32
        )
    ).astype(jnp.bfloat16)[None]
    return (grad_tokens, grad_router, grad_win, out_weight_gradient)


def solution(mesh):
    return jax.shard_map(
        body,
        mesh=mesh,
        in_specs=(
            P(("dp", "tok", "expert"), None, None),
            P(),
            P(("tok", "expert"), None, "dp"),
            P(("tok", "expert"), "dp", None),
            P(("dp", "tok", "expert"), None, None),
        ),
        out_specs=(
            P(("dp", "tok", "expert"), None, None),
            P(),
            P(("tok", "expert"), None, "dp"),
            P(("tok", "expert"), "dp", None),
        ),
        check_vma=False,
    )
```

```python
import jax
import jax.numpy as jnp
from jax import lax
from jax.sharding import PartitionSpec as P

ITERS = 4


GELU_SCALE = 0.7978845608028654
GELU_CUBIC = 0.044715


def gelu_pair(hidden_pre):
    inner_arg = GELU_SCALE * (hidden_pre + GELU_CUBIC * hidden_pre * hidden_pre * hidden_pre)
    tanh_val = jnp.tanh(inner_arg)
    activated = 0.5 * hidden_pre * (1.0 + tanh_val)
    derivative = 0.5 * (1.0 + tanh_val) + 0.5 * hidden_pre * (
        1.0 - tanh_val * tanh_val
    ) * GELU_SCALE * (1.0 + 3.0 * GELU_CUBIC * hidden_pre * hidden_pre)
    return (activated, derivative)


def forward_iterates(router_scores):
    iterate = router_scores
    stored_residuals = []
    for sweep_index in range(ITERS):
        line_divisor_factor = iterate - jax.nn.logsumexp(iterate, axis=1, keepdims=True)
        column_divisor = line_divisor_factor - jax.nn.logsumexp(
            line_divisor_factor, axis=0, keepdims=True
        )
        stored_residuals.append((line_divisor_factor, column_divisor))
        iterate = column_divisor
    return stored_residuals


def backward_sequence(gradient, stored_residuals):
    for line_divisor_factor, column_divisor in reversed(stored_residuals):
        gradient = gradient - jnp.exp(column_divisor) * jnp.sum(gradient, axis=0, keepdims=True)
        gradient = gradient - jnp.exp(line_divisor_factor) * jnp.sum(
            gradient, axis=1, keepdims=True
        )
    return gradient


def shift(value, step):
    size = lax.axis_size("dp")
    return lax.ppermute(value, "dp", [(i, (i + step) % size) for i in range(size)])


def gather_blocks(rows):
    half = rows.shape[1] // 2
    behind_two, ahead_two = shift(rows, 2), shift(rows, -2)
    behind_one, ahead_one = shift(rows, 1), shift(rows, -1)
    behind_three, ahead_three = shift(behind_two, 1), shift(ahead_two, -1)
    away = jnp.concatenate(
        [shift(behind_two[:, :half], 2), shift(ahead_two[:, half:], -2)], axis=1
    )
    return jnp.concatenate(
        [rows, behind_one, ahead_one, behind_two, ahead_two, behind_three, ahead_three, away], axis=0
    )


def reduce_blocks(partial, rows):
    half = partial.shape[1] // 2
    block = [partial[i * rows : (i + 1) * rows] for i in range(8)]
    own, behind_one, ahead_one, behind_two, ahead_two, behind_three, ahead_three, away = block
    send = lambda value, step: shift(value.astype(jnp.bfloat16), step).astype(jnp.float32)
    down, up = send(behind_three, -1), send(ahead_three, 1)
    away_down, away_up = send(away[:, :half], -2), send(away[:, half:], 2)
    near = send(behind_one, -1) + send(ahead_one, 1)
    down, up = down + behind_two, up + ahead_two
    down = jnp.concatenate([down[:, :half] + away_down, down[:, half:]], axis=1)
    up = jnp.concatenate([up[:, :half], up[:, half:] + away_up], axis=1)
    return own + near + (send(down, -2) + send(up, 2))


def swap(value):
    return lax.all_to_all(value, ("tok", "expert"), split_axis=0, concat_axis=0, tiled=True)


def sum_everywhere(part):
    slots, width = part.shape
    halves = part.astype(jnp.bfloat16).reshape(slots, 2, width // 2)
    mine = jnp.sum(swap(halves).astype(jnp.float32), axis=0, keepdims=True)
    copies = jnp.broadcast_to(mine, (lax.axis_size("dp"), 2, width // 2))
    seen = lax.all_to_all(copies, "dp", split_axis=0, concat_axis=0, tiled=True)
    total = jnp.sum(seen, axis=0, keepdims=True).astype(jnp.bfloat16)
    everywhere = swap(jnp.broadcast_to(total, (slots, 2, width // 2)))
    return everywhere.reshape(slots, width).astype(jnp.float32)


def paired_swap(first, second):
    moved = swap(jnp.stack([first, second], axis=1))
    return jnp.concatenate([moved[:, 0], moved[:, 1]], axis=1)


def body(tokens, router, expert_in, expert_out, grad_out):
    patches, image_grad = tokens[0], grad_out[0]
    model_width = patches.shape[1]
    router_scores = jnp.dot(patches, router, preferred_element_type=jnp.float32)
    combine = jax.nn.softmax(router_scores, axis=1)
    combine_rounded = combine.astype(jnp.bfloat16)
    stored_residuals = forward_iterates(router_scores)
    assignment_matrix = jnp.exp(stored_residuals[-1][1])
    dispatch_rounded = assignment_matrix.astype(jnp.bfloat16)
    slot_part = jnp.dot(dispatch_rounded.T, patches, preferred_element_type=jnp.float32).astype(
        jnp.bfloat16
    )
    grad_part = jnp.dot(combine_rounded.T, image_grad, preferred_element_type=jnp.float32).astype(
        jnp.bfloat16
    )
    rows = paired_swap(slot_part, grad_part)
    gathered = gather_blocks(rows)
    all_in, all_grad = gathered[:, :model_width], gathered[:, model_width:]
    weight_in = expert_in[0]
    weight_out = expert_out[0]
    hidden_pre = jnp.dot(all_in, weight_in, preferred_element_type=jnp.float32)
    activated, derivative = gelu_pair(hidden_pre)
    hidden_act = activated.astype(jnp.bfloat16)
    grad_act = lax.dot_general(
        all_grad, weight_out, (((1,), (1,)), ((), ())), preferred_element_type=jnp.float32
    )
    grad_pre = (grad_act * derivative).astype(jnp.bfloat16)
    forward_rows = jnp.dot(hidden_act, weight_out, preferred_element_type=jnp.float32)
    backward_rows = lax.dot_general(
        grad_pre, weight_in, (((1,), (1,)), ((), ())), preferred_element_type=jnp.float32
    )
    summed = reduce_blocks(
        jnp.concatenate([forward_rows, backward_rows], axis=1), rows.shape[0]
    ).astype(jnp.bfloat16)
    grad_win = lax.dot_general(
        all_in, grad_pre, (((0,), (0,)), ((), ())), preferred_element_type=jnp.float32
    ).astype(jnp.bfloat16)[None]
    out_weight_gradient = lax.dot_general(
        hidden_act, all_grad, (((0,), (0,)), ((), ())), preferred_element_type=jnp.float32
    ).astype(jnp.bfloat16)[None]
    back = paired_swap(summed[:, :model_width], summed[:, model_width:])
    back_out, back_grad = back[:, :model_width], back[:, model_width:]
    grad_comb = lax.dot_general(
        image_grad, back_out, (((1,), (1,)), ((), ())), preferred_element_type=jnp.float32
    )
    logit_cotangent = combine * (grad_comb - jnp.sum(combine * grad_comb, axis=1, keepdims=True))
    doubly_stochastic_adjoint = (
        lax.dot_general(
            patches, back_grad, (((1,), (1,)), ((), ())), preferred_element_type=jnp.float32
        )
        * assignment_matrix
    )
    doubly_stochastic_adjoint = backward_sequence(doubly_stochastic_adjoint, stored_residuals)
    accumulated_cotangent = (logit_cotangent + doubly_stochastic_adjoint).astype(jnp.bfloat16)
    router_part = lax.dot_general(
        accumulated_cotangent, patches, (((0,), (0,)), ((), ())), preferred_element_type=jnp.float32
    )
    grad_router = sum_everywhere(router_part).T
    grad_tokens = (
        jnp.dot(dispatch_rounded, back_grad, preferred_element_type=jnp.float32)
        + lax.dot_general(
            accumulated_cotangent, router, (((1,), (1,)), ((), ())), preferred_element_type=jnp.float32
        )
    ).astype(jnp.bfloat16)[None]
    return (grad_tokens, grad_router, grad_win, out_weight_gradient)


def solution(mesh):
    return jax.shard_map(
        body,
        mesh=mesh,
        in_specs=(
            P(("dp", "tok", "expert"), None, None),
            P(),
            P(("tok", "expert"), None, "dp"),
            P(("tok", "expert"), "dp", None),
            P(("dp", "tok", "expert"), None, None),
        ),
        out_specs=(
            P(("dp", "tok", "expert"), None, None),
            P(),
            P(("tok", "expert"), None, "dp"),
            P(("tok", "expert"), "dp", None),
        ),
        check_vma=False,
    )
```

```python
import jax
import jax.numpy as jnp
from jax import lax
from jax.sharding import PartitionSpec as P

ITERS = 4


GELU_SCALE = 0.7978845608028654
GELU_CUBIC = 0.044715


def gelu_pair(hidden_pre):
    inner_arg = GELU_SCALE * (hidden_pre + GELU_CUBIC * hidden_pre * hidden_pre * hidden_pre)
    tanh_val = jnp.tanh(inner_arg)
    activated = 0.5 * hidden_pre * (1.0 + tanh_val)
    derivative = 0.5 * (1.0 + tanh_val) + 0.5 * hidden_pre * (
        1.0 - tanh_val * tanh_val
    ) * GELU_SCALE * (1.0 + 3.0 * GELU_CUBIC * hidden_pre * hidden_pre)
    return (activated, derivative)


def log_sum_exp(value, axis):
    highest = jnp.max(value, axis=axis, keepdims=True)
    return highest + jnp.log(jnp.sum(jnp.exp(value - highest), axis=axis, keepdims=True))


def forward_iterates(router_scores):
    iterate = router_scores
    stored_residuals = []
    for sweep_index in range(ITERS):
        line_divisor_factor = iterate - log_sum_exp(iterate, 1)
        column_divisor = line_divisor_factor - log_sum_exp(line_divisor_factor, 0)
        stored_residuals.append((line_divisor_factor, column_divisor))
        iterate = column_divisor
    return stored_residuals


def backward_sequence(gradient, stored_residuals):
    for line_divisor_factor, column_divisor in reversed(stored_residuals):
        gradient = gradient - jnp.exp(column_divisor) * jnp.sum(gradient, axis=0, keepdims=True)
        gradient = gradient - jnp.exp(line_divisor_factor) * jnp.sum(
            gradient, axis=1, keepdims=True
        )
    return gradient


def shift(value, step):
    size = lax.axis_size("dp")
    return lax.ppermute(value, "dp", [(i, (i + step) % size) for i in range(size)])


def gather_blocks(rows):
    half = rows.shape[1] // 2
    behind_two, ahead_two = shift(rows, 2), shift(rows, -2)
    behind_one, ahead_one = shift(rows, 1), shift(rows, -1)
    behind_three, ahead_three = shift(behind_two, 1), shift(ahead_two, -1)
    away = jnp.concatenate(
        [shift(behind_two[:, :half], 2), shift(ahead_two[:, half:], -2)], axis=1
    )
    return jnp.concatenate(
        [rows, behind_one, ahead_one, behind_two, ahead_two, behind_three, ahead_three, away], axis=0
    )


def reduce_blocks(partial, rows):
    half = partial.shape[1] // 2
    block = [partial[i * rows : (i + 1) * rows] for i in range(8)]
    own, behind_one, ahead_one, behind_two, ahead_two, behind_three, ahead_three, away = block
    send = lambda value, step: shift(value.astype(jnp.bfloat16), step).astype(jnp.float32)
    down, up = send(behind_three, -1), send(ahead_three, 1)
    away_down, away_up = send(away[:, :half], -2), send(away[:, half:], 2)
    near = send(behind_one, -1) + send(ahead_one, 1)
    down, up = down + behind_two, up + ahead_two
    down = jnp.concatenate([down[:, :half] + away_down, down[:, half:]], axis=1)
    up = jnp.concatenate([up[:, :half], up[:, half:] + away_up], axis=1)
    return own + near + (send(down, -2) + send(up, 2))


def swap(value):
    return lax.all_to_all(value, ("tok", "expert"), split_axis=0, concat_axis=0, tiled=True)


def sum_everywhere(part):
    slots, width = part.shape
    halves = part.astype(jnp.bfloat16).reshape(slots, 2, width // 2)
    mine = jnp.sum(swap(halves).astype(jnp.float32), axis=0, keepdims=True)
    copies = jnp.broadcast_to(mine, (lax.axis_size("dp"), 2, width // 2))
    seen = lax.all_to_all(copies, "dp", split_axis=0, concat_axis=0, tiled=True)
    total = jnp.sum(seen, axis=0, keepdims=True).astype(jnp.bfloat16)
    everywhere = swap(jnp.broadcast_to(total, (slots, 2, width // 2)))
    return everywhere.reshape(slots, width).astype(jnp.float32)


def paired_swap(first, second):
    moved = swap(jnp.stack([first, second], axis=1))
    return jnp.concatenate([moved[:, 0], moved[:, 1]], axis=1)


def body(tokens, router, expert_in, expert_out, grad_out):
    patches, image_grad = tokens[0], grad_out[0]
    model_width = patches.shape[1]
    router_scores = jnp.dot(patches, router, preferred_element_type=jnp.float32)
    stored_residuals = forward_iterates(router_scores)
    combine = jnp.exp(stored_residuals[0][0])
    combine_rounded = combine.astype(jnp.bfloat16)
    assignment_matrix = jnp.exp(stored_residuals[-1][1])
    dispatch_rounded = assignment_matrix.astype(jnp.bfloat16)
    slot_part = jnp.dot(dispatch_rounded.T, patches, preferred_element_type=jnp.float32).astype(
        jnp.bfloat16
    )
    grad_part = jnp.dot(combine_rounded.T, image_grad, preferred_element_type=jnp.float32).astype(
        jnp.bfloat16
    )
    rows = paired_swap(slot_part, grad_part)
    gathered = gather_blocks(rows)
    all_in, all_grad = gathered[:, :model_width], gathered[:, model_width:]
    weight_in = expert_in[0]
    weight_out = expert_out[0]
    hidden_pre = jnp.dot(all_in, weight_in, preferred_element_type=jnp.float32)
    activated, derivative = gelu_pair(hidden_pre)
    hidden_act = activated.astype(jnp.bfloat16)
    grad_act = lax.dot_general(
        all_grad, weight_out, (((1,), (1,)), ((), ())), preferred_element_type=jnp.float32
    )
    grad_pre = (grad_act * derivative).astype(jnp.bfloat16)
    forward_rows = jnp.dot(hidden_act, weight_out, preferred_element_type=jnp.float32)
    backward_rows = lax.dot_general(
        grad_pre, weight_in, (((1,), (1,)), ((), ())), preferred_element_type=jnp.float32
    )
    summed = reduce_blocks(
        jnp.concatenate([forward_rows, backward_rows], axis=1), rows.shape[0]
    ).astype(jnp.bfloat16)
    grad_win = lax.dot_general(
        all_in, grad_pre, (((0,), (0,)), ((), ())), preferred_element_type=jnp.float32
    ).astype(jnp.bfloat16)[None]
    out_weight_gradient = lax.dot_general(
        hidden_act, all_grad, (((0,), (0,)), ((), ())), preferred_element_type=jnp.float32
    ).astype(jnp.bfloat16)[None]
    back = paired_swap(summed[:, :model_width], summed[:, model_width:])
    back_out, back_grad = back[:, :model_width], back[:, model_width:]
    grad_comb = lax.dot_general(
        image_grad, back_out, (((1,), (1,)), ((), ())), preferred_element_type=jnp.float32
    )
    logit_cotangent = combine * (grad_comb - jnp.sum(combine * grad_comb, axis=1, keepdims=True))
    doubly_stochastic_adjoint = (
        lax.dot_general(
            patches, back_grad, (((1,), (1,)), ((), ())), preferred_element_type=jnp.float32
        )
        * assignment_matrix
    )
    doubly_stochastic_adjoint = backward_sequence(doubly_stochastic_adjoint, stored_residuals)
    accumulated_cotangent = (logit_cotangent + doubly_stochastic_adjoint).astype(jnp.bfloat16)
    router_part = lax.dot_general(
        accumulated_cotangent, patches, (((0,), (0,)), ((), ())), preferred_element_type=jnp.float32
    )
    grad_router = sum_everywhere(router_part).T
    grad_tokens = (
        jnp.dot(dispatch_rounded, back_grad, preferred_element_type=jnp.float32)
        + lax.dot_general(
            accumulated_cotangent, router, (((1,), (1,)), ((), ())), preferred_element_type=jnp.float32
        )
    ).astype(jnp.bfloat16)[None]
    return (grad_tokens, grad_router, grad_win, out_weight_gradient)


def solution(mesh):
    return jax.shard_map(
        body,
        mesh=mesh,
        in_specs=(
            P(("dp", "tok", "expert"), None, None),
            P(),
            P(("tok", "expert"), None, "dp"),
            P(("tok", "expert"), "dp", None),
            P(("dp", "tok", "expert"), None, None),
        ),
        out_specs=(
            P(("dp", "tok", "expert"), None, None),
            P(),
            P(("tok", "expert"), None, "dp"),
            P(("tok", "expert"), "dp", None),
        ),
        check_vma=False,
    )
```
